32 devices in a mesh: bus: 2 (over y), line: 2 (over x), scen: 8 (over z, core).
Axes of the slice: x: 2, y: 2, z: 4, core: 2. Of those that a mesh axis runs over, the one named last changes fastest.
Arguments:
- shift_factors: bfloat16 [12288, 8192], P('line', 'bus'), may hold values from -0.0625 to 0.0625
- net_load: bfloat16 [512, 8, 8192], P('scen', None, 'bus'), may hold values from -6 to 6
- dispatch_level: float32 [512, 8], P('scen'), may hold values from 0.3 to 1.5
- scenario_weight: float32 [512], P('scen'), may hold values from 0.5 to 2
- cluster_id: int32 [512, 1], P('scen'), may hold values from 0 to 63
- commitment: int32 [8, 4096], P(None, 'bus'), may hold values 0 or 1
- unit_capacity: float32 [4096], P('bus'), may hold values from 0.5 to 4
- unit_bus: int32 [4096], P('bus'), may hold values from 0 to 8191
- line_limit: float32 [12288], P('line'), may hold values from 0.3 to 1.5
- multipliers: float32 [64, 12288], P('scen', 'line'), may hold values from 0 to 1
- penalty_target: float32 [64], P('scen'), may hold values from 1 to 16
Outputs:
- new_multipliers: float32 [64, 12288], P('scen', 'line')
- cut_slopes: float32 [64, 8, 8192], P(('line', 'scen'), None, 'bus')
The draws below stay inside these ranges and needn't reach their ends.
All inputs are finite; a program needn't handle non-finite values. No bound on the sum of `commitment` on one device may be relied on, other than what follows from the above.
Results may differ from the reference program's by a relative error of at most 0.0011.
Values may be sent and summed in bfloat16 or wider, within the bound.
A program may use at most 128 MiB of HBM per device.

```python
import math
import jax
import jax.numpy as jnp
from jax import lax

BUSES = 8192
LINES = 12288
GENS = 4096
CLUSTERS = 64
HOURS = 8
SCEN = 512


def with_ends(entries, stream_key, least, largest):
    shape = entries.shape
    spot = [jax.random.randint(jax.random.fold_in(stream_key, axis), (), 0, shape[axis]) for axis in range(len(shape))]
    entries = entries.at[tuple(spot)].set(least)
    longest = shape.index(max(shape))
    spot[longest] = (spot[longest] + 1) % shape[longest]
    return entries.at[tuple(spot)].set(largest)


def level_of(own_key, dims, shards, least, largest):
    factor_of, own = 1.0, jax.random.fold_in(own_key, 6)
    for axis_at, parts in shards:
        draws = jnp.exp(jax.random.uniform(jax.random.fold_in(own, axis_at), (parts,), jnp.float32, least / len(shards), largest / len(shards)))
        factor_of = factor_of * jnp.repeat(draws, dims[axis_at] // parts).reshape([-1 if axis == axis_at else 1 for axis in range(len(dims))])
    return factor_of


def different_ones(key, rows, amount, top, lift):
    order = jax.random.permutation(jax.random.fold_in(key, 1), amount)
    favour = order
    for power in range(3):
        favour = favour * favour // amount
    favour = favour * lift // amount
    chance = jax.random.randint(jax.random.fold_in(key, 2), (rows, amount), 0, 4096) + favour
    fixed_rows = jax.random.permutation(jax.random.fold_in(key, 3), rows)[jnp.arange(amount) % rows]
    chance = jnp.where(jnp.arange(rows)[:, None] == fixed_rows[None, :], 1 << 14, chance)
    priority = chance * amount + jnp.arange(amount)
    return lax.top_k(priority.astype(jnp.int32), top)[1].astype(jnp.int32)


def gaussian(key, dims, spread, limit, pieces=(), kind=jnp.bfloat16):
    entries = jax.random.normal(key, dims, jnp.float32) * spread
    if len(pieces) > 0:
        entries = level_of(key, dims, pieces, -0.22, 0.18) * entries
    return jnp.clip(entries, min=-limit, max=limit).astype(kind)


def setup_inputs(seed: int = 0) -> dict:
    keys = jax.random.split(jax.random.key(seed), 12)
    return {
        "shift_factors": gaussian(keys[0], (LINES, BUSES), BUSES ** -0.5, 0.0625, ((0, 2), (1, 2))),
        "net_load": gaussian(keys[1], (SCEN, HOURS, BUSES), 1.0, 6.0, ((0, 8), (2, 2))),
        "dispatch_level": jnp.clip(jnp.exp(math.log(1.5) - 1.60943787 * jax.random.uniform(keys[2], (SCEN, HOURS), jnp.float32) ** level_of(keys[2], (SCEN, HOURS), ((0, 8),), -0.2, 0.2)), 0.3, 1.5),
        "scenario_weight": jnp.clip(jnp.exp(math.log(2.0) - 1.3862944 * jax.random.uniform(keys[3], (SCEN,), jnp.float32) ** level_of(keys[3], (SCEN,), ((0, 8),), -0.2, 0.2)), 0.5, 2.0),
        "cluster_id": different_ones(keys[4], SCEN, CLUSTERS, 1, 256),
        "commitment": with_ends((jax.random.randint(keys[5], (HOURS, GENS), 0, 4) < 3).astype(jnp.int32), jax.random.fold_in(keys[5], 1), 0, 1),
        "unit_capacity": jnp.clip(jnp.exp(math.log(4.0) - 2.0794415 * jax.random.uniform(keys[6], (GENS,), jnp.float32) ** level_of(keys[6], (GENS,), ((0, 2),), -0.2, 0.2)), 0.5, 4.0),
        "unit_bus": with_ends(jax.random.randint(keys[7], (GENS,), 0, BUSES), jax.random.fold_in(keys[7], 1), 0, BUSES - 1).astype(jnp.int32),
        "line_limit": jnp.clip(0.3 + 1.2 * jax.random.uniform(keys[8], (LINES,), jnp.float32) ** level_of(keys[8], (LINES,), ((0, 2),), -0.2, 0.2), 0.3, 1.5),
        "multipliers": jnp.clip(1.0 * jax.random.uniform(keys[9], (CLUSTERS, LINES), jnp.float32) ** level_of(keys[9], (CLUSTERS, LINES), ((0, 8), (1, 2)), -0.2, 0.2), 0.0, 1.0),
        "penalty_target": jnp.clip(jnp.exp(math.log(16.0) - 2.7725887 * jax.random.uniform(keys[10], (CLUSTERS,), jnp.float32) ** level_of(keys[10], (CLUSTERS,), ((0, 8),), -0.2, 0.2)), 1.0, 16.0),
    }


step_size = 0.1


def reference(shift_factors, net_load, dispatch_level, scenario_weight, cluster_id, commitment, unit_capacity, unit_bus, line_limit, multipliers, penalty_target):
    highest = lax.Precision.HIGHEST
    values = commitment.astype(jnp.float32) * unit_capacity[None, :]
    capacity = jax.ops.segment_sum(values.T, unit_bus, num_segments=BUSES).T
    injection = (capacity[None, :, :] * dispatch_level[:, :, None] - net_load.astype(jnp.float32)).astype(jnp.bfloat16)
    factors = shift_factors.astype(jnp.float32)
    inject_flat = injection.reshape(SCEN * HOURS, BUSES).astype(jnp.float32)
    flow = lax.dot_general(factors, inject_flat, (((1,), (1,)), ((), ())), precision=highest)
    flow_cube = flow.reshape(LINES, SCEN, HOURS)
    bounds = line_limit[:, None, None]
    excess = flow_cube - jnp.clip(flow_cube, -bounds, bounds)
    penalty = 0.5 * jnp.sum(excess * excess, axis=2) * scenario_weight[None, :]
    member = (cluster_id[:, 0:1] == jnp.arange(CLUSTERS).astype(jnp.int32)[None, :]).astype(jnp.float32)
    pooled = jnp.dot(member.T, penalty.T, precision=highest)
    new_multipliers = jnp.maximum(multipliers + step_size * (pooled - penalty_target[:, None]), 0.0)
    chosen = jnp.dot(member, new_multipliers, precision=highest)
    push = (excess * (chosen.T * scenario_weight[None, :])[:, :, None]).astype(jnp.bfloat16)
    push_flat = push.reshape(LINES, SCEN * HOURS).astype(jnp.float32)
    sensitivity = lax.dot_general(push_flat, factors, (((0,), (0,)), ((), ())), precision=highest)
    scaled = (sensitivity.reshape(SCEN, HOURS, BUSES) * dispatch_level[:, :, None]).reshape(SCEN, HOURS * BUSES)
    cut_slopes = jnp.dot(member.T, scaled, precision=highest).reshape(CLUSTERS, HOURS, BUSES)
    return new_multipliers, cut_slopes
```

```python
import jax
import jax.numpy as jnp
from jax import lax
from jax.sharding import PartitionSpec as P

step_size = 0.1
LANES = 128


def shift_by(axis, amount):
    size = lax.axis_size(axis)
    return [(i, (i + amount) % size) for i in range(size)]


def halves(x):
    high = lax.reduce_precision(x, 8, 7)
    return high.astype(jnp.bfloat16), (x - high).astype(jnp.bfloat16)


def pick(x, index, axis=0):
    return lax.dynamic_index_in_dim(x, index, axis, keepdims=False)


def scatter_sum(parts, axis, kind):
    size, me = lax.axis_size(axis), lax.axis_index(axis)
    total = pick(parts, me)
    for d in range(1, size):
        sent = pick(parts, (me + d) % size).astype(kind)
        total = total + lax.ppermute(sent, axis, shift_by(axis, d)).astype(jnp.float32)
    return total


def gather(part, axis):
    size, me = lax.axis_size(axis), lax.axis_index(axis)
    if size == 2:
        other = lax.ppermute(part, axis, shift_by(axis, 1))
        first = jnp.where(me == 0, part, other)
        second = jnp.where(me == 0, other, part)
        return jnp.stack([first, second])
    return lax.all_gather(part, axis, axis=0)


def per_device(
    shift_factors,
    net_load,
    dispatch_level,
    scenario_weight,
    cluster_id,
    commitment,
    unit_capacity,
    unit_bus,
    line_limit,
    multipliers,
    penalty_target,
):
    highest, high = lax.Precision.HIGHEST, lax.Precision.HIGH
    f32, bf16 = jnp.float32, jnp.bfloat16
    lines, buses = shift_factors.shape
    scens, hours, _ = net_load.shape
    columns = scens * hours
    nb, nl, ns = lax.axis_size("bus"), lax.axis_size("line"), lax.axis_size("scen")
    me_b, me_l, me_s = lax.axis_index("bus"), lax.axis_index("line"), lax.axis_index("scen")
    own = multipliers.shape[0]
    clusters = own * ns
    group = clusters // (nl * ns)
    chunks = max([k for k in (1, 2, 4) if lines % (k * nb * LANES) == 0] or [1])
    width = lines // chunks
    sub = width // nb

    values = commitment.astype(f32) * unit_capacity[None, :]
    tops = nb * buses // LANES
    top = unit_bus // LANES == jnp.arange(tops, dtype=jnp.int32)[:, None]
    low = (unit_bus % LANES)[:, None] == jnp.arange(LANES, dtype=jnp.int32)[None, :]
    placed = jnp.where(top[None], values[:, None, :], 0.0).reshape(hours * tops, -1)
    spread = jnp.dot(placed, low.astype(f32), precision=highest)
    spread = spread.reshape(hours, nb, buses // LANES, LANES).transpose(1, 0, 2, 3)
    capacity = scatter_sum(spread, "bus", f32).reshape(hours, buses)
    injection = (
        capacity[None] * dispatch_level[:, :, None] - net_load.astype(f32)
    ).astype(bf16).reshape(columns, buses)

    owner, hour_row, slot, place = (
        lax.broadcasted_iota(jnp.int32, (ns, hours, nl, group), i) for i in range(4)
    )
    row_cluster = ((slot * ns + owner) * group + place).reshape(-1)
    row_hour = hour_row.reshape(-1)
    scen_of = jnp.repeat(cluster_id[:, 0], hours)
    weight_of = jnp.repeat(scenario_weight, hours)
    hour_of = jnp.tile(jnp.arange(hours, dtype=jnp.int32), scens)
    same = (row_cluster[:, None] == scen_of[None, :]) & (row_hour[:, None] == hour_of[None, :])
    pool = jnp.where(same, (weight_of * dispatch_level.reshape(-1))[None, :], 0.0)
    penalty_cluster = row_cluster.reshape(ns, hours, own)[:, 0].reshape(-1)
    penalty_pool = jnp.where(
        penalty_cluster[:, None] == scen_of[None, :], 0.5 * weight_of[None, :], 0.0
    )

    limits = pick(line_limit.reshape(chunks, nb, sub), me_b, 1)
    current = pick(multipliers.reshape(own, chunks, nb, sub), me_b, 2)
    everyone = lax.all_gather(current, "scen", axis=0)
    current = pick(everyone.reshape(nl, ns, group, chunks, sub), me_s, 1).reshape(own, chunks, sub)
    targets = lax.all_gather(penalty_target, "scen", axis=0)
    targets = pick(targets.reshape(nl, ns, group), me_s, 1).reshape(own)

    pairs = ns // 2
    swap = [(i, i ^ 1) for i in range(ns)]
    me_pair, me_side = me_s // 2, me_s % 2
    duals, slopes = [], None
    received = []
    for k in range(chunks):
        part = lax.dot_general(
            injection,
            shift_factors[k * width : (k + 1) * width],
            (((1,), (1,)), ((), ())),
            preferred_element_type=f32,
        )
        part = part.reshape(columns, nb, sub).transpose(1, 0, 2)
        received.append(scatter_sum(part, "bus", bf16))
    for k in range(chunks):
        flow = received[k]
        edge = limits[k][None, :]
        excess = flow - jnp.clip(flow, -edge, edge)
        pooled = jnp.dot(pool, excess, precision=high)
        penalty = jnp.dot(penalty_pool, excess * excess, precision=high)
        both = jnp.concatenate(
            [pooled.reshape(ns, hours * own, sub), penalty.reshape(ns, own, sub)], axis=1
        ).reshape(pairs, 2, (hours + 1) * own, sub)
        both = pick(both, me_side, 1) + lax.ppermute(pick(both, 1 - me_side, 1), "scen", swap)
        total = pick(both, me_pair)
        cut = hours * own
        for d in range(1, pairs):
            sent = pick(both, (me_pair + d) % pairs)
            sent = jnp.concatenate([sent[:cut].astype(bf16), *halves(sent[cut:])], axis=0)
            perm = [(i, (i + 2 * d) % ns) for i in range(ns)]
            came = lax.ppermute(sent, "scen", perm).astype(f32)
            total = total + jnp.concatenate(
                [came[:cut], came[cut : cut + own] + came[cut + own :]], axis=0
            )
        dual = jnp.maximum(
            current[:, k] + step_size * (total[cut:] - targets[:, None]), 0.0
        )
        duals.append(dual)
        pushed = total[:cut].reshape(hours, own, sub) * dual[None]
        pushed = pushed.transpose(1, 0, 2).reshape(own * hours, sub)
        packed = gather(jnp.concatenate(halves(pushed), axis=0), "bus")
        packed = packed.transpose(1, 0, 2).reshape(2 * own * hours, width)
        step = jnp.dot(
            packed, shift_factors[k * width : (k + 1) * width], preferred_element_type=f32
        )
        slopes = step if slopes is None else slopes + step
    slopes = slopes[: own * hours] + slopes[own * hours :]
    slopes = scatter_sum(slopes.reshape(nl, group, hours, buses), "line", f32)

    dual = jnp.stack(duals, axis=1).reshape(own, chunks * sub)
    every = lax.all_gather(dual, "scen", axis=0).reshape(ns, nl, group, chunks * sub)
    every = every.transpose(1, 0, 2, 3).reshape(ns, own, chunks * sub)
    mine = gather(pick(every, me_s), "bus").reshape(nb, own, chunks, sub)
    dual_out = mine.transpose(1, 2, 0, 3).reshape(own, lines)
    return dual_out, slopes


def solution(mesh):
    placed = (
        P("line", "bus"),
        P("scen", None, "bus"),
        P("scen", None),
        P("scen"),
        P("scen", None),
        P(None, "bus"),
        P("bus"),
        P("bus"),
        P("line"),
        P("scen", "line"),
        P("scen"),
    )
    return jax.shard_map(
        per_device,
        mesh=mesh,
        in_specs=placed,
        out_specs=(P("scen", "line"), P(("line", "scen"), None, "bus")),
        check_vma=False,
    )
```
